32 devices in a mesh: dp: 16 (over z, y, x), zero: 2 (over core).
Axes of the slice: x: 2, y: 2, z: 4, core: 2. Of those that a mesh axis runs over, the one named last changes fastest.
Arguments:
- tokens: bfloat16 [8192, 768], P(('dp', 'zero')), may hold values from -6 to 6
- cotangent: bfloat16 [8192, 768], P(('dp', 'zero')), may hold values from -6 to 6
- segment_ids: int32 [32, 256], P(('dp', 'zero')), may hold values from 0 to 5, never falling along the last dimension, each value on 1 to 128 neighbouring positions
- packed_weights: float32 [768, 6144], P(None, ('dp', 'zero')), may hold values from -0.5412659 to 0.5412659
- down_weights: float32 [3072, 768], P(('dp', 'zero')), may hold values from -0.109375 to 0.109375
- vector_params: float32 [13, 768], P(None, 'zero'), may hold values from -1.5 to 3.5, as said below
- packed_first: float32 [768, 6144], P(None, ('dp', 'zero')), may hold values from -6.788225 to 6.788225
- packed_second: float32 [768, 6144], P(None, ('dp', 'zero')), may hold values from 0.32768 to 66.3552
- down_first: float32 [3072, 768], P(('dp', 'zero')), may hold values from -16 to 16
- down_second: float32 [3072, 768], P(('dp', 'zero')), may hold values from 16.384 to 163.84
- vector_first: float32 [13, 768], P(None, 'zero'), may hold values from -28 to 28
- vector_second: float32 [13, 768], P(None, 'zero'), may hold values from 40.96 to 409.6
Outputs:
- block_output: bfloat16 [8192, 768], P(('dp', 'zero'))
- tokens_grad: float32 [8192, 768], P(('dp', 'zero'))
- packed_grad: float32 [768, 6144], P(None, ('dp', 'zero'))
- down_grad: float32 [3072, 768], P(('dp', 'zero'))
- vector_grad: float32 [13, 768], P(None, 'zero')
- packed_new: float32 [768, 6144], P(None, ('dp', 'zero'))
- down_new: float32 [3072, 768], P(('dp', 'zero'))
- vector_step: float32 [13, 768], P(None, 'zero')
- packed_first_new: float32 [768, 6144], P(None, ('dp', 'zero'))
- packed_second_new: float32 [768, 6144], P(None, ('dp', 'zero'))
- down_first_new: float32 [3072, 768], P(('dp', 'zero'))
- down_second_new: float32 [3072, 768], P(('dp', 'zero'))
- vector_first_new: float32 [13, 768], P(None, 'zero')
- vector_second_new: float32 [13, 768], P(None, 'zero')
The draws below stay inside these ranges and needn't reach their ends.
Inputs may be any that keep to these rules, and one draw needn't show every extreme that they name: `segment_ids`: each row holds 6 sequences numbered in order, each of 1 to 128 slots, one of exactly 128. `vector_params`: rows 0 and 2 are positive.
All inputs are finite; a program needn't handle non-finite values.
Results may differ from the reference program's by a relative error of at most 0.0025.
The reference program's roundings to bfloat16 on the way (of `probs_low`, `attended_low`, `activated`, `grad_attended_low` and `grad_scores_low`) count: a program that leaves them out, or rounds other values in their place, can miss the bound.
Values may be sent and summed in bfloat16 or wider, within the bound.
A program may use at most 192 MiB of HBM per device.

```python
import math
import jax
import jax.numpy as jnp
import numpy as np
from jax import lax

D = 768
FF = 3072
H = 12
HEAD = 64
ROT = 16
TOK_DEV = 256
SEQS_DEV = 6
STEP_COUNT = 4
SEQ_MAX = 128
VROWS = 13
TOKENS = 8192
N_DP = 16
N_ZERO = 2


def column_scales(qkv_part, out_part, up_part):
    column = jnp.arange(4 * D + FF)
    return jnp.where(column < 3 * D, qkv_part, jnp.where(column < 4 * D, out_part, up_part))[None, :]


def draw_packed_weights(key, part):
    key = jax.random.fold_in(key, 11)
    shape_full = (D, 4 * D + FF)
    sample = jnp.clip(jax.random.normal(key, shape_full, jnp.float32), -5.0, 5.0)
    return sample * column_scales(1.0, 3.0, 1.0) / jnp.sqrt(D * 1.0)


def draw_vector_params(key, part):
    key = jax.random.fold_in(key, 12)
    row_total = 9 + FF // D
    sample = jnp.clip(jax.random.normal(key, (row_total, D), jnp.float32), -5.0, 5.0)
    row_index = jnp.arange(row_total)[:, None]
    is_gain = (row_index == 0) | (row_index == 2)
    return jnp.where(is_gain, jnp.exp(0.25 * sample), 0.3 * sample)


def draw_packed_first(key, part):
    key = jax.random.fold_in(key, 13)
    shape_full = (D, 4 * D + FF)
    sample = jnp.clip(jax.random.normal(key, shape_full, jnp.float32), -5.0, 5.0)
    return sample * column_scales(0.1, 0.3, 0.25) * 0.05 * jnp.sqrt(TOKENS * 1.0)


def draw_packed_second(key, part):
    key = jax.random.fold_in(key, 14)
    shape_full = (D, 4 * D + FF)
    spread = jnp.exp(jax.random.uniform(key, shape_full, jnp.float32, -1.5, 1.5))
    return spread * column_scales(0.01, 0.09, 0.0625) * 0.02 * (TOKENS * 1.0)


def level_of(stream_key, dims, cuts, smallest, top_value):
    gain = 1.0
    for position, parts in cuts:
        steps = jax.random.uniform(jax.random.fold_in(jax.random.fold_in(stream_key, 6), position), (parts,), jnp.float32, smallest / len(cuts), top_value / len(cuts))
        gain = gain * jnp.repeat(jnp.exp(steps), dims[position] // parts).reshape((-1,) + (1,) * (len(dims) - 1 - position))
    return gain


def length_profile(number_of, total, bound, slope):
    loads = [(1 << 20) // math.isqrt(grade ** slope) + 1 for grade in range(2, number_of + 1)]
    spare, given = total - bound - (number_of - 1), [1] * (number_of - 1)
    while spare > 0:
        candidates = [i for i in range(number_of - 1) if given[i] < bound]
        pool, remaining = sum([loads[i] for i in candidates]), spare
        for i in candidates:
            addition = min(bound - given[i], max(1, remaining * loads[i] // pool), spare)
            given[i] = given[i] + addition
            spare = spare - addition
    return np.array([bound] + given)


def uneven(stream_key, number_of, total, reach, skew):
    if number_of == 2:
        one = jax.random.randint(stream_key, (), max(1, total - reach), min(reach, total - 1) + 1)
        return jnp.stack([one, total - one])
    tallies = jnp.asarray(length_profile(number_of, total, reach, skew), jnp.int32)
    twos = (number_of - 1) // 2
    giver, taker = tallies[1:1 + 2 * twos:2], tallies[2:2 + 2 * twos:2]
    slack = jnp.minimum(giver - 1, reach - taker)
    passed = jax.random.randint(jax.random.fold_in(stream_key, 1), (twos,), 0, 1 << 20) % (slack + 1)
    tallies = tallies.at[1:1 + 2 * twos:2].set(giver - passed).at[2:2 + 2 * twos:2].set(taker + passed)
    return tallies[jax.random.permutation(jax.random.fold_in(stream_key, 2), number_of)]


def gaussian(own_key, dims, width, limit, shards=(), kind=jnp.bfloat16):
    entries = jax.random.normal(own_key, dims, jnp.float32) * width
    if len(shards) > 0:
        entries = level_of(own_key, dims, shards, -0.22, 0.18) * entries
    return jnp.clip(entries, min=-limit, max=limit).astype(kind)


def setup_inputs(seed: int = 0) -> dict:
    arg_keys = jax.random.split(jax.random.key(seed), 13)
    return {
        "tokens": gaussian(arg_keys[0], (TOKENS, D), 1.0, 6.0, ((0, 32),)),
        "cotangent": gaussian(arg_keys[1], (TOKENS, D), 1.0, 6.0, ((0, 32),)),
        "segment_ids": jax.vmap(lambda own: jnp.searchsorted(jnp.cumsum(uneven(own, SEQS_DEV, TOK_DEV, SEQ_MAX, 2)), jnp.arange(TOK_DEV), side="right"))(jax.random.split(arg_keys[2], (N_DP * N_ZERO))).reshape((N_DP * N_ZERO, TOK_DEV)).astype(jnp.int32),
        "packed_weights": draw_packed_weights(jax.random.fold_in(arg_keys[12], 71), 0),
        "down_weights": gaussian(arg_keys[4], (FF, D), FF ** -0.5, 0.109375, ((0, 32),), jnp.float32),
        "vector_params": draw_vector_params(jax.random.fold_in(arg_keys[12], 71), 0),
        "packed_first": draw_packed_first(jax.random.fold_in(arg_keys[12], 71), 0),
        "packed_second": draw_packed_second(jax.random.fold_in(arg_keys[12], 71), 0),
        "down_first": gaussian(arg_keys[8], (FF, D), (0.03 * TOKENS ** 0.5), 16.0, ((0, 32),), jnp.float32),
        "down_second": jnp.clip(jnp.exp(math.log(163.84) - 2.30258502 * jax.random.uniform(arg_keys[9], (FF, D), jnp.float32) ** level_of(arg_keys[9], (FF, D), ((0, 32),), -0.2, 0.2)), 16.384, 163.84),
        "vector_first": gaussian(arg_keys[10], (VROWS, D), (0.05 * TOKENS ** 0.5), 28.0, ((1, 2),), jnp.float32),
        "vector_second": jnp.clip(jnp.exp(math.log(409.6) - 2.3025851 * jax.random.uniform(arg_keys[11], (VROWS, D), jnp.float32) ** level_of(arg_keys[11], (VROWS, D), ((1, 2),), -0.2, 0.2)), 40.96, 409.6),
    }


norm_epsilon = 1e-05
adam_epsilon = 1e-08
learn_rate = 0.01
decay_rate = 0.1
beta_first = 0.9
beta_second = 0.95
rope_base = 10000.0
masked_value = -1e+30
inv_sqrt_two = 0.7071067811865476
inv_sqrt_tau = 0.3989422804014327

def contract(form, left, right):
    return jnp.einsum(form, left.astype(jnp.float32), right.astype(jnp.float32))

def layer_norm(residual, gain_vector, bias_vector):
    centered = residual - lax.optimization_barrier(jnp.mean(residual, axis=-1, keepdims=True))
    inverse = lax.rsqrt(lax.optimization_barrier(jnp.mean(centered * centered, axis=-1, keepdims=True)) + norm_epsilon)
    normalized = centered * inverse
    return (normalized * gain_vector + bias_vector, normalized, inverse)

def norm_backward(grad_normed, normalized, inverse, gain_vector):
    grad_gain = lax.optimization_barrier(jnp.sum(grad_normed * normalized, axis=0))
    grad_bias = lax.optimization_barrier(jnp.sum(grad_normed, axis=0))
    grad_hat = grad_normed * gain_vector
    grad_input = inverse * (grad_hat - lax.optimization_barrier(jnp.mean(grad_hat, axis=-1, keepdims=True)) - normalized * lax.optimization_barrier(jnp.mean(grad_hat * normalized, axis=-1, keepdims=True)))
    return (grad_input, grad_gain, grad_bias)

def rotary_tables(segment_row):
    row_count = segment_row.shape[0]
    positions_all = jnp.arange(row_count, dtype=jnp.int32)
    same_segment = segment_row[:, None] == segment_row[None, :]
    starts = lax.optimization_barrier(jnp.min(jnp.where(same_segment, positions_all[None, :], row_count), axis=1))
    offsets = (positions_all - starts).astype(jnp.float32)
    half_rot = ROT // 2
    frequency = jnp.power(rope_base, -(jnp.arange(half_rot, dtype=jnp.float32) * 2.0 / ROT))
    angles = offsets[:, None] * frequency[None, :]
    allowed = same_segment & (positions_all[None, :] <= positions_all[:, None])
    return (jnp.cos(angles)[:, None, :], jnp.sin(angles)[:, None, :], allowed)

def rotate_heads(values, cosine, sine_table):
    half_rot = ROT // 2
    front = values[..., :half_rot]
    behind = values[..., half_rot:ROT]
    return jnp.concatenate([front * cosine - behind * sine_table, behind * cosine + front * sine_table, values[..., ROT:]], axis=-1)

def gelu_parts(upward):
    normal_cdf = 0.5 * (1.0 + lax.erf(upward * inv_sqrt_two))
    density = jnp.exp(-0.5 * upward * upward) * inv_sqrt_tau
    return (upward * normal_cdf, normal_cdf + upward * density)

def layer_rows(token_rows, cotangent_rows, segment_row, packed_low, down_low, vector_low):
    row_count, model_width = token_rows.shape
    ffn_width = down_low.shape[0]
    vector_full = vector_low.astype(jnp.float32)
    residual = token_rows.astype(jnp.float32)
    normed_one, unit_one, inverse_one = layer_norm(residual, vector_full[0], vector_full[1])
    normed_two, unit_two, inverse_two = layer_norm(residual, vector_full[2], vector_full[3])
    normed_one_low = normed_one.astype(jnp.bfloat16)
    normed_two_low = normed_two.astype(jnp.bfloat16)
    weight_qkv = packed_low[:, :3 * model_width]
    weight_out = packed_low[:, 3 * model_width:4 * model_width]
    weight_up = packed_low[:, 4 * model_width:]
    bias_qkv = vector_full[6:9].reshape(3 * model_width)
    bias_up = vector_full[9:].reshape(ffn_width)
    projected = jnp.dot(normed_one_low, weight_qkv, preferred_element_type=jnp.float32) + bias_qkv
    heads_shape = (row_count, H, HEAD)
    cosine, sine_table, allowed = rotary_tables(segment_row)
    query_low = rotate_heads(projected[:, :model_width].reshape(heads_shape), cosine, sine_table).astype(jnp.bfloat16)
    key_low = rotate_heads(projected[:, model_width:2 * model_width].reshape(heads_shape), cosine, sine_table).astype(jnp.bfloat16)
    value_low = projected[:, 2 * model_width:].reshape(heads_shape).astype(jnp.bfloat16)
    score_scale = HEAD ** (-0.5)

    def attention_scores():
        scores = contract('qhd,khd->hqk', query_low, key_low) * score_scale
        return jnp.where(allowed[None], scores, masked_value)
    scores = attention_scores()
    log_total = jnp.log(lax.optimization_barrier(jnp.sum(jnp.exp(scores), axis=-1, keepdims=True)))
    probs_low = jnp.exp(scores - log_total).astype(jnp.bfloat16)
    attended = contract('hqk,khd->qhd', probs_low, value_low)
    attended_low = attended.reshape(row_count, model_width).astype(jnp.bfloat16)
    branch_attn = jnp.dot(attended_low, weight_out, preferred_element_type=jnp.float32) + vector_full[4]
    upward = jnp.dot(normed_two_low, weight_up, preferred_element_type=jnp.float32) + bias_up
    activated, gelu_slope = gelu_parts(upward)
    activated_low = activated.astype(jnp.bfloat16)
    branch_mlp = jnp.dot(activated_low, down_low, preferred_element_type=jnp.float32) + vector_full[5]
    block_output = (residual + branch_attn + branch_mlp).astype(jnp.bfloat16)
    grad_rows = cotangent_rows.astype(jnp.float32)
    grad_bias_rows = lax.optimization_barrier(jnp.sum(grad_rows, axis=0))
    grad_down = jnp.dot(activated_low.T, cotangent_rows, preferred_element_type=jnp.float32)
    grad_upward = jnp.dot(cotangent_rows, down_low.T, preferred_element_type=jnp.float32) * gelu_slope
    grad_upward_low = grad_upward.astype(jnp.bfloat16)
    grad_weight_up = jnp.dot(normed_two_low.T, grad_upward_low, preferred_element_type=jnp.float32)
    grad_normed_two = jnp.dot(grad_upward_low, weight_up.T, preferred_element_type=jnp.float32)
    grad_weight_out = jnp.dot(attended_low.T, cotangent_rows, preferred_element_type=jnp.float32)
    grad_attended_low = jnp.dot(cotangent_rows, weight_out.T, preferred_element_type=jnp.float32).astype(jnp.bfloat16).reshape(heads_shape)
    correction = lax.optimization_barrier(jnp.sum(grad_attended_low.astype(jnp.float32) * attended, axis=-1))
    attention_probs = jnp.exp(attention_scores() - log_total)
    grad_probs = contract('qhd,khd->hqk', grad_attended_low, value_low)
    grad_scores_low = (attention_probs * (grad_probs - correction.T[:, :, None]) * score_scale).astype(jnp.bfloat16)
    probs_again = attention_probs.astype(jnp.bfloat16)
    grad_query = contract('hqk,khd->qhd', grad_scores_low, key_low)
    grad_key = contract('hqk,qhd->khd', grad_scores_low, query_low)
    grad_value = contract('hqk,qhd->khd', probs_again, grad_attended_low)
    grad_projected = jnp.concatenate([rotate_heads(grad_query, cosine, -sine_table).reshape(row_count, model_width), rotate_heads(grad_key, cosine, -sine_table).reshape(row_count, model_width), grad_value.reshape(row_count, model_width)], axis=1)
    grad_projected_low = grad_projected.astype(jnp.bfloat16)
    grad_weight_qkv = jnp.dot(normed_one_low.T, grad_projected_low, preferred_element_type=jnp.float32)
    grad_normed_one = jnp.dot(grad_projected_low, weight_qkv.T, preferred_element_type=jnp.float32)
    input_one, gain_one, bias_one = norm_backward(grad_normed_one, unit_one, inverse_one, vector_full[0])
    input_two, gain_two, bias_two = norm_backward(grad_normed_two, unit_two, inverse_two, vector_full[2])
    grad_tokens = grad_rows + input_one + input_two
    grad_packed = jnp.concatenate([grad_weight_qkv, grad_weight_out, grad_weight_up], axis=1)
    grad_vector = jnp.concatenate([jnp.stack([gain_one, bias_one, gain_two, bias_two, grad_bias_rows, grad_bias_rows]), lax.optimization_barrier(jnp.sum(grad_projected, axis=0)).reshape(3, model_width), lax.optimization_barrier(jnp.sum(grad_upward, axis=0)).reshape(ffn_width // model_width, model_width)], axis=0)
    return (block_output, grad_tokens, grad_packed, grad_down, grad_vector)

def adam_moments(first_moment, second, grad_total):
    first_new = beta_first * first_moment + (1.0 - beta_first) * grad_total
    second_new = beta_second * second + (1.0 - beta_second) * grad_total * grad_total
    first_hat = first_new / (1.0 - beta_first ** STEP_COUNT)
    second_hat = second_new / (1.0 - beta_second ** STEP_COUNT)
    return (first_new, second_new, first_hat / (jnp.sqrt(second_hat) + adam_epsilon))

def adam_update(weight, first_moment, second, grad_total):
    first_new, second_new, direction = adam_moments(first_moment, second, grad_total)
    weight_new = weight * (1.0 - learn_rate * decay_rate) - learn_rate * direction
    return (weight_new, first_new, second_new)

def adam_change(weight, first_moment, second, grad_total):
    first_new, second_new, direction = adam_moments(first_moment, second, grad_total)
    change = -(learn_rate * decay_rate) * weight - learn_rate * direction
    return (change, first_new, second_new)

def reference(tokens, cotangent, segment_ids, packed_weights, down_weights, vector_params, packed_first, packed_second, down_first, down_second, vector_first, vector_second):
    rank_count = N_DP * N_ZERO
    packed_low = packed_weights.astype(jnp.bfloat16)
    down_low = down_weights.astype(jnp.bfloat16)
    vector_low = vector_params.astype(jnp.bfloat16)
    token_blocks = tokens.reshape(rank_count, TOK_DEV, D)
    cotangent_blocks = cotangent.reshape(rank_count, TOK_DEV, D)

    def visit(totals, inputs):
        token_rows, cotangent_rows, segment_row = inputs
        block_output, grad_tokens, grad_packed, grad_down, grad_vector = layer_rows(token_rows, cotangent_rows, segment_row, packed_low, down_low, vector_low)
        return ((totals[0] + grad_packed, totals[1] + grad_down, totals[2] + grad_vector), (block_output, grad_tokens))
    start_totals = (jnp.zeros(packed_weights.shape, jnp.float32), jnp.zeros(down_weights.shape, jnp.float32), jnp.zeros(vector_params.shape, jnp.float32))
    (packed_grad, down_grad, vector_grad), (outputs, input_grads) = lax.scan(visit, start_totals, (token_blocks, cotangent_blocks, segment_ids))
    packed_new, packed_first_new, packed_second_new = adam_update(packed_weights, packed_first, packed_second, packed_grad)
    down_new, down_first_new, down_second_new = adam_update(down_weights, down_first, down_second, down_grad)
    vector_step, vector_first_new, vector_second_new = adam_change(vector_params, vector_first, vector_second, vector_grad)
    return (outputs.reshape(TOKENS, D), input_grads.reshape(TOKENS, D), packed_grad, down_grad, vector_grad, packed_new, down_new, vector_step, packed_first_new, packed_second_new, down_first_new, down_second_new, vector_first_new, vector_second_new)
```

```python
import functools

import jax
import jax.numpy as jnp
from jax import lax
from jax.sharding import PartitionSpec as P

H = 12
HEAD = 64
ROT = 16
STEP_COUNT = 4


norm_epsilon = 1e-05
adam_epsilon = 1e-08
learn_rate = 0.01
decay_rate = 0.1
beta_first = 0.9
beta_second = 0.95
rope_base = 10000.0
masked_value = -1e30
inv_sqrt_two = 0.7071067811865476
inv_sqrt_tau = 0.3989422804014327


def contract(form, left, right):
    return jnp.einsum(form, left, right, preferred_element_type=jnp.float32)


def layer_norm(residual, gain_vector, bias_vector):
    centered = residual - jnp.mean(residual, axis=-1, keepdims=True)
    inverse = lax.rsqrt(jnp.mean(centered * centered, axis=-1, keepdims=True) + norm_epsilon)
    normalized = centered * inverse
    return (normalized * gain_vector + bias_vector, normalized, inverse)


def norm_backward(grad_normed, normalized, inverse, gain_vector):
    grad_gain = jnp.sum(grad_normed * normalized, axis=0)
    grad_bias = jnp.sum(grad_normed, axis=0)
    grad_hat = grad_normed * gain_vector
    grad_input = inverse * (
        grad_hat
        - jnp.mean(grad_hat, axis=-1, keepdims=True)
        - normalized * jnp.mean(grad_hat * normalized, axis=-1, keepdims=True)
    )
    return (grad_input, grad_gain, grad_bias)


def rotary_tables(segment_row):
    row_count = segment_row.shape[0]
    positions_all = jnp.arange(row_count, dtype=jnp.int32)
    same_segment = segment_row[:, None] == segment_row[None, :]
    starts = jnp.min(jnp.where(same_segment, positions_all[None, :], row_count), axis=1)
    offsets = (positions_all - starts).astype(jnp.float32)
    half_rot = ROT // 2
    frequency = jnp.power(rope_base, -(jnp.arange(half_rot, dtype=jnp.float32) * 2.0 / ROT))
    angles = offsets[:, None] * frequency[None, :]
    allowed = same_segment & (positions_all[None, :] <= positions_all[:, None])
    return (jnp.cos(angles)[:, None, :], jnp.sin(angles)[:, None, :], allowed)


def rotate_heads(values, cosine, sine_table):
    half_rot = ROT // 2
    front = values[..., :half_rot]
    behind = values[..., half_rot:ROT]
    return jnp.concatenate(
        [
            front * cosine - behind * sine_table,
            behind * cosine + front * sine_table,
            values[..., ROT:],
        ],
        axis=-1,
    )


def gelu_parts(upward):
    normal_cdf = 0.5 * (1.0 + lax.erf(upward * inv_sqrt_two))
    density = jnp.exp(-0.5 * upward * upward) * inv_sqrt_tau
    return (upward * normal_cdf, normal_cdf + upward * density)


def layer_rows(token_rows, cotangent_rows, segment_row, packed_low, down_low, vector_low):
    row_count, model_width = token_rows.shape
    ffn_width = down_low.shape[0]
    vector_full = vector_low.astype(jnp.float32)
    residual = token_rows.astype(jnp.float32)
    normed_one, unit_one, inverse_one = layer_norm(residual, vector_full[0], vector_full[1])
    normed_two, unit_two, inverse_two = layer_norm(residual, vector_full[2], vector_full[3])
    normed_one_low = normed_one.astype(jnp.bfloat16)
    normed_two_low = normed_two.astype(jnp.bfloat16)
    weight_qkv = packed_low[: 3 * model_width].T
    weight_out = packed_low[3 * model_width : 4 * model_width].T
    weight_up = packed_low[4 * model_width :].T
    bias_qkv = vector_full[6:9].reshape(3 * model_width)
    bias_up = vector_full[9:].reshape(ffn_width)
    projected = jnp.dot(normed_one_low, weight_qkv, preferred_element_type=jnp.float32) + bias_qkv
    heads_shape = (row_count, H, HEAD)
    cosine, sine_table, allowed = rotary_tables(segment_row)
    query_low = rotate_heads(
        projected[:, :model_width].reshape(heads_shape), cosine, sine_table
    ).astype(jnp.bfloat16)
    key_low = rotate_heads(
        projected[:, model_width : 2 * model_width].reshape(heads_shape), cosine, sine_table
    ).astype(jnp.bfloat16)
    value_low = projected[:, 2 * model_width :].reshape(heads_shape).astype(jnp.bfloat16)
    score_scale = HEAD ** (-0.5)

    def attention_scores():
        scores = contract("qhd,khd->hqk", query_low, key_low) * score_scale
        return jnp.where(allowed[None], scores, masked_value)

    scores = attention_scores()
    log_total = jnp.log(jnp.sum(jnp.exp(scores), axis=-1, keepdims=True))
    probs_low = jnp.exp(scores - log_total).astype(jnp.bfloat16)
    attended = contract("hqk,khd->qhd", probs_low, value_low)
    attended_low = attended.reshape(row_count, model_width).astype(jnp.bfloat16)
    branch_attn = (
        jnp.dot(attended_low, weight_out, preferred_element_type=jnp.float32) + vector_full[4]
    )
    upward = jnp.dot(normed_two_low, weight_up, preferred_element_type=jnp.float32) + bias_up
    activated, gelu_slope = gelu_parts(upward)
    activated_low = activated.astype(jnp.bfloat16)
    branch_mlp = (
        jnp.dot(activated_low, down_low, preferred_element_type=jnp.float32) + vector_full[5]
    )
    block_output = (residual + branch_attn + branch_mlp).astype(jnp.bfloat16)
    grad_rows = cotangent_rows.astype(jnp.float32)
    grad_bias_rows = jnp.sum(grad_rows, axis=0)
    grad_down = jnp.dot(activated_low.T, cotangent_rows, preferred_element_type=jnp.float32)
    grad_upward = (
        jnp.dot(cotangent_rows, down_low.T, preferred_element_type=jnp.float32) * gelu_slope
    )
    grad_upward_low = grad_upward.astype(jnp.bfloat16)
    grad_weight_up = jnp.dot(grad_upward_low.T, normed_two_low, preferred_element_type=jnp.float32)
    grad_normed_two = jnp.dot(grad_upward_low, weight_up.T, preferred_element_type=jnp.float32)
    grad_weight_out = jnp.dot(cotangent_rows.T, attended_low, preferred_element_type=jnp.float32)
    grad_attended_low = (
        jnp.dot(cotangent_rows, weight_out.T, preferred_element_type=jnp.float32)
        .astype(jnp.bfloat16)
        .reshape(heads_shape)
    )
    correction = jnp.sum(grad_attended_low.astype(jnp.float32) * attended, axis=-1)
    attention_probs = jnp.exp(attention_scores() - log_total)
    grad_probs = contract("qhd,khd->hqk", grad_attended_low, value_low)
    grad_scores_low = (
        attention_probs * (grad_probs - correction.T[:, :, None]) * score_scale
    ).astype(jnp.bfloat16)
    probs_again = attention_probs.astype(jnp.bfloat16)
    grad_query = contract("hqk,khd->qhd", grad_scores_low, key_low)
    grad_key = contract("hqk,qhd->khd", grad_scores_low, query_low)
    grad_value = contract("hqk,qhd->khd", probs_again, grad_attended_low)
    grad_projected = jnp.concatenate(
        [
            rotate_heads(grad_query, cosine, -sine_table).reshape(row_count, model_width),
            rotate_heads(grad_key, cosine, -sine_table).reshape(row_count, model_width),
            grad_value.reshape(row_count, model_width),
        ],
        axis=1,
    )
    grad_projected_low = grad_projected.astype(jnp.bfloat16)
    grad_weight_qkv = jnp.dot(
        grad_projected_low.T, normed_one_low, preferred_element_type=jnp.float32
    )
    grad_normed_one = jnp.dot(grad_projected_low, weight_qkv.T, preferred_element_type=jnp.float32)
    input_one, gain_one, bias_one = norm_backward(
        grad_normed_one, unit_one, inverse_one, vector_full[0]
    )
    input_two, gain_two, bias_two = norm_backward(
        grad_normed_two, unit_two, inverse_two, vector_full[2]
    )
    grad_tokens = grad_rows + input_one + input_two
    grad_packed = [grad_weight_qkv, grad_weight_out, grad_weight_up]
    grad_vector = jnp.concatenate(
        [
            jnp.stack([gain_one, bias_one, gain_two, bias_two, grad_bias_rows, grad_bias_rows]),
            jnp.sum(grad_projected, axis=0).reshape(3, model_width),
            jnp.sum(grad_upward, axis=0).reshape(ffn_width // model_width, model_width),
        ],
        axis=0,
    )
    return (block_output, grad_tokens, grad_packed, grad_down, grad_vector)


def adam_moments(first_moment, second, grad_total):
    first_new = beta_first * first_moment + (1.0 - beta_first) * grad_total
    second_new = beta_second * second + (1.0 - beta_second) * grad_total * grad_total
    first_hat = first_new / (1.0 - beta_first**STEP_COUNT)
    second_hat = second_new / (1.0 - beta_second**STEP_COUNT)
    return (first_new, second_new, first_hat / (jnp.sqrt(second_hat) + adam_epsilon))


def adam_update(weight, first_moment, second, grad_total):
    first_new, second_new, direction = adam_moments(first_moment, second, grad_total)
    weight_new = weight * (1.0 - learn_rate * decay_rate) - learn_rate * direction
    return (weight_new, first_new, second_new)


def adam_change(weight, first_moment, second, grad_total):
    first_new, second_new, direction = adam_moments(first_moment, second, grad_total)
    change = -(learn_rate * decay_rate) * weight - learn_rate * direction
    return (change, first_new, second_new)


AXES = ("dp", "zero")


def exchange(value, size, mask):
    return lax.ppermute(value, AXES, [(i, i ^ mask) for i in range(size)])


def stage_lists(bit_count):
    rest = [(3, 4)] if bit_count >= 5 else [(b,) for b in range(3, bit_count)]
    rest = rest + [(b,) for b in range(5, bit_count)]
    return [[(1,), (2,)] + rest, [(2,), (1,)] + rest]


def scatter_stage(value, present, group, me, size, wire):
    span = 1 << len(group)
    low = group[0]
    mine = (me >> low) & (span - 1)
    top = group[-1]
    axis = present.index(top)
    shape = value.shape
    value = value.reshape(shape[:axis] + (span,) + shape[axis + len(group) :])
    total = lax.dynamic_index_in_dim(value, mine, axis, keepdims=False)
    for k in range(1, span):
        part = lax.dynamic_index_in_dim(value, mine ^ k, axis, keepdims=False).astype(wire)
        total = total + exchange(part, size, k << low).astype(jnp.float32)
    return total, [b for b in present if b not in group]


def scatter_parts(parts, me, size):
    rows = sum(p.shape[0] for p in parts) // size
    width = parts[0].shape[1]
    bit_count = size.bit_length() - 1
    core = me & 1
    split = [p.reshape(p.shape[0] // (2 * rows), 2, rows, width) for p in parts]
    pieces = []
    half = width // 2
    for index, stages in enumerate(stage_lists(bit_count)):
        cut = [p[..., index * half : (index + 1) * half] for p in split]
        send = jnp.concatenate(
            [lax.dynamic_index_in_dim(p, 1 - core, 1, keepdims=False) for p in cut], axis=0
        )
        keep = jnp.concatenate(
            [lax.dynamic_index_in_dim(p, core, 1, keepdims=False) for p in cut], axis=0
        )
        value = keep + exchange(send, size, 1)
        present = list(range(bit_count - 1, 0, -1))
        value = value.reshape((2,) * (bit_count - 1) + (rows, half))
        for group in stages:
            wire = jnp.bfloat16 if group in ((1,), (2,)) else jnp.float32
            value, present = scatter_stage(value, present, group, me, size, wire)
        pieces.append(value)
    return jnp.concatenate(pieces, axis=-1)


def gather_rows(shard, me, size):
    rows, width = shard.shape
    bit_count = size.bit_length() - 1
    half = width // 2
    pieces = []
    for index, stages in enumerate(stage_lists(bit_count)):
        value = shard[:, index * half : (index + 1) * half]
        present = []
        for group in list(reversed(stages)) + [(0,)]:
            span = 1 << len(group)
            low = group[0]
            slots = [value] + [exchange(value, size, k << low) for k in range(1, span)]
            for t, b in enumerate(group):
                bit = ((me >> b) & 1) == 1
                slots = [jnp.where(bit, slots[j ^ (1 << t)], slots[j]) for j in range(span)]
            axis = sum(1 for b in present if b > group[-1])
            value = jnp.stack(slots, axis=axis)
            value = value.reshape(
                value.shape[:axis] + (2,) * len(group) + value.shape[axis + 1 :]
            )
            present = sorted(present + list(group), reverse=True)
        pieces.append(value.reshape(size * rows, half))
    return jnp.concatenate(pieces, axis=-1)


def reduce_vector(grad_vector, me, size, zero_size):
    bit_count = size.bit_length() - 1
    total = grad_vector
    for b in range(bit_count):
        total = total + exchange(total, size, 1 << b)
    width = grad_vector.shape[1] // zero_size
    return lax.dynamic_slice_in_dim(total, (me % zero_size) * width, width, axis=1)


def body(
    zero_size,
    size,
    tokens,
    cotangent,
    segment_ids,
    packed_weights,
    down_weights,
    vector_params,
    packed_first,
    packed_second,
    down_first,
    down_second,
    vector_first,
    vector_second,
):
    me = lax.axis_index("dp") * zero_size + lax.axis_index("zero")
    packed_shard = packed_weights.astype(jnp.bfloat16).T
    down_shard = down_weights.astype(jnp.bfloat16)
    vector_shard = vector_params.astype(jnp.bfloat16)
    packed_full = gather_rows(packed_shard, me, size)
    down_full = gather_rows(down_shard, me, size)
    vector_full = lax.all_gather(vector_shard, "zero", axis=1, tiled=True)
    block_output, grad_tokens, grad_packed, grad_down, grad_vector = layer_rows(
        tokens, cotangent, segment_ids[0], packed_full, down_full, vector_full
    )
    down_sum = scatter_parts([grad_down], me, size)
    packed_sum = scatter_parts(grad_packed, me, size).T
    vector_sum = reduce_vector(grad_vector, me, size, zero_size)
    packed_new, packed_first_new, packed_second_new = adam_update(
        packed_weights, packed_first, packed_second, packed_sum
    )
    down_new, down_first_new, down_second_new = adam_update(
        down_weights, down_first, down_second, down_sum
    )
    vector_step, vector_first_new, vector_second_new = adam_change(
        vector_params, vector_first, vector_second, vector_sum
    )
    return (
        block_output,
        grad_tokens,
        packed_sum,
        down_sum,
        vector_sum,
        packed_new,
        down_new,
        vector_step,
        packed_first_new,
        packed_second_new,
        down_first_new,
        down_second_new,
        vector_first_new,
        vector_second_new,
    )


def solution(mesh):
    zero_size = mesh.shape["zero"]
    size = mesh.shape["dp"] * zero_size
    return jax.shard_map(
        functools.partial(body, zero_size, size),
        mesh=mesh,
        in_specs=(
            P(("dp", "zero"), None),
            P(("dp", "zero"), None),
            P(("dp", "zero"), None),
            P(None, ("dp", "zero")),
            P(("dp", "zero"), None),
            P(None, "zero"),
            P(None, ("dp", "zero")),
            P(None, ("dp", "zero")),
            P(("dp", "zero"), None),
            P(("dp", "zero"), None),
            P(None, "zero"),
            P(None, "zero"),
        ),
        out_specs=(
            P(("dp", "zero"), None),
            P(("dp", "zero"), None),
            P(None, ("dp", "zero")),
            P(("dp", "zero"), None),
            P(None, "zero"),
            P(None, ("dp", "zero")),
            P(("dp", "zero"), None),
            P(None, "zero"),
            P(None, ("dp", "zero")),
            P(None, ("dp", "zero")),
            P(("dp", "zero"), None),
            P(("dp", "zero"), None),
            P(None, "zero"),
            P(None, "zero"),
        ),
        check_vma=False,
    )
```

```python
import functools

import jax
import jax.numpy as jnp
from jax import lax
from jax.sharding import PartitionSpec as P

H = 12
HEAD = 64
ROT = 16
STEP_COUNT = 4


norm_epsilon = 1e-05
adam_epsilon = 1e-08
learn_rate = 0.01
decay_rate = 0.1
beta_first = 0.9
beta_second = 0.95
rope_base = 10000.0
masked_value = -1e30
inv_sqrt_two = 0.7071067811865476
inv_sqrt_tau = 0.3989422804014327


def contract(form, left, right):
    return jnp.einsum(form, left, right, preferred_element_type=jnp.float32)


def layer_norm(residual, gain_vector, bias_vector):
    centered = residual - jnp.mean(residual, axis=-1, keepdims=True)
    inverse = lax.rsqrt(jnp.mean(centered * centered, axis=-1, keepdims=True) + norm_epsilon)
    normalized = centered * inverse
    return (normalized * gain_vector + bias_vector, normalized, inverse)


def norm_backward(grad_normed, normalized, inverse, gain_vector):
    grad_gain = jnp.sum(grad_normed * normalized, axis=0)
    grad_bias = jnp.sum(grad_normed, axis=0)
    grad_hat = grad_normed * gain_vector
    grad_input = inverse * (
        grad_hat
        - jnp.mean(grad_hat, axis=-1, keepdims=True)
        - normalized * jnp.mean(grad_hat * normalized, axis=-1, keepdims=True)
    )
    return (grad_input, grad_gain, grad_bias)


def rotary_tables(segment_row):
    row_count = segment_row.shape[0]
    positions_all = jnp.arange(row_count, dtype=jnp.int32)
    same_segment = segment_row[:, None] == segment_row[None, :]
    starts = jnp.min(jnp.where(same_segment, positions_all[None, :], row_count), axis=1)
    offsets = (positions_all - starts).astype(jnp.float32)
    half_rot = ROT // 2
    frequency = jnp.power(rope_base, -(jnp.arange(half_rot, dtype=jnp.float32) * 2.0 / ROT))
    angles = offsets[:, None] * frequency[None, :]
    allowed = same_segment & (positions_all[None, :] <= positions_all[:, None])
    return (jnp.cos(angles)[:, None, :], jnp.sin(angles)[:, None, :], allowed)


def rotate_heads(values, cosine, sine_table):
    half_rot = ROT // 2
    front = values[..., :half_rot]
    behind = values[..., half_rot:ROT]
    return jnp.concatenate(
        [
            front * cosine - behind * sine_table,
            behind * cosine + front * sine_table,
            values[..., ROT:],
        ],
        axis=-1,
    )


def gelu_parts(upward):
    normal_cdf = 0.5 * (1.0 + lax.erf(upward * inv_sqrt_two))
    density = jnp.exp(-0.5 * upward * upward) * inv_sqrt_tau
    return (upward * normal_cdf, normal_cdf + upward * density)


def layer_rows(token_rows, cotangent_rows, segment_row, packed_low, down_low, vector_low):
    row_count, model_width = token_rows.shape
    ffn_width = down_low.shape[0]
    vector_full = vector_low.astype(jnp.float32)
    residual = token_rows.astype(jnp.float32)
    normed_one, unit_one, inverse_one = layer_norm(residual, vector_full[0], vector_full[1])
    normed_two, unit_two, inverse_two = layer_norm(residual, vector_full[2], vector_full[3])
    normed_one_low = normed_one.astype(jnp.bfloat16)
    normed_two_low = normed_two.astype(jnp.bfloat16)
    weight_qkv = packed_low[: 3 * model_width].T
    weight_out = packed_low[3 * model_width : 4 * model_width].T
    weight_up = packed_low[4 * model_width :].T
    bias_qkv = vector_full[6:9].reshape(3 * model_width)
    bias_up = vector_full[9:].reshape(ffn_width)
    upward = jnp.dot(normed_two_low, weight_up, preferred_element_type=jnp.float32) + bias_up
    activated, gelu_slope = gelu_parts(upward)
    activated_low = activated.astype(jnp.bfloat16)
    grad_down = jnp.dot(activated_low.T, cotangent_rows, preferred_element_type=jnp.float32)
    grad_upward = (
        jnp.dot(cotangent_rows, down_low.T, preferred_element_type=jnp.float32) * gelu_slope
    )
    grad_upward_low = grad_upward.astype(jnp.bfloat16)
    grad_weight_up = jnp.dot(grad_upward_low.T, normed_two_low, preferred_element_type=jnp.float32)
    normed_one_low, grad_down, grad_weight_up = lax.optimization_barrier(
        (normed_one_low, grad_down, grad_weight_up)
    )
    projected = jnp.dot(normed_one_low, weight_qkv, preferred_element_type=jnp.float32) + bias_qkv
    heads_shape = (row_count, H, HEAD)
    cosine, sine_table, allowed = rotary_tables(segment_row)
    query_low = rotate_heads(
        projected[:, :model_width].reshape(heads_shape), cosine, sine_table
    ).astype(jnp.bfloat16)
    key_low = rotate_heads(
        projected[:, model_width : 2 * model_width].reshape(heads_shape), cosine, sine_table
    ).astype(jnp.bfloat16)
    value_low = projected[:, 2 * model_width :].reshape(heads_shape).astype(jnp.bfloat16)
    score_scale = HEAD ** (-0.5)

    def attention_scores():
        scores = contract("qhd,khd->hqk", query_low, key_low) * score_scale
        return jnp.where(allowed[None], scores, masked_value)

    scores = attention_scores()
    log_total = jnp.log(jnp.sum(jnp.exp(scores), axis=-1, keepdims=True))
    probs_low = jnp.exp(scores - log_total).astype(jnp.bfloat16)
    attended = contract("hqk,khd->qhd", probs_low, value_low)
    attended_low = attended.reshape(row_count, model_width).astype(jnp.bfloat16)
    branch_attn = (
        jnp.dot(attended_low, weight_out, preferred_element_type=jnp.float32) + vector_full[4]
    )
    branch_mlp = (
        jnp.dot(activated_low, down_low, preferred_element_type=jnp.float32) + vector_full[5]
    )
    block_output = (residual + branch_attn + branch_mlp).astype(jnp.bfloat16)
    grad_rows = cotangent_rows.astype(jnp.float32)
    grad_bias_rows = jnp.sum(grad_rows, axis=0)
    grad_normed_two = jnp.dot(grad_upward_low, weight_up.T, preferred_element_type=jnp.float32)
    grad_weight_out = jnp.dot(cotangent_rows.T, attended_low, preferred_element_type=jnp.float32)
    grad_attended_low = (
        jnp.dot(cotangent_rows, weight_out.T, preferred_element_type=jnp.float32)
        .astype(jnp.bfloat16)
        .reshape(heads_shape)
    )
    correction = jnp.sum(grad_attended_low.astype(jnp.float32) * attended, axis=-1)
    attention_probs = jnp.exp(attention_scores() - log_total)
    grad_probs = contract("qhd,khd->hqk", grad_attended_low, value_low)
    grad_scores_low = (
        attention_probs * (grad_probs - correction.T[:, :, None]) * score_scale
    ).astype(jnp.bfloat16)
    probs_again = attention_probs.astype(jnp.bfloat16)
    grad_query = contract("hqk,khd->qhd", grad_scores_low, key_low)
    grad_key = contract("hqk,qhd->khd", grad_scores_low, query_low)
    grad_value = contract("hqk,qhd->khd", probs_again, grad_attended_low)
    grad_projected = jnp.concatenate(
        [
            rotate_heads(grad_query, cosine, -sine_table).reshape(row_count, model_width),
            rotate_heads(grad_key, cosine, -sine_table).reshape(row_count, model_width),
            grad_value.reshape(row_count, model_width),
        ],
        axis=1,
    )
    grad_projected_low = grad_projected.astype(jnp.bfloat16)
    grad_weight_qkv = jnp.dot(
        grad_projected_low.T, normed_one_low, preferred_element_type=jnp.float32
    )
    grad_normed_one = jnp.dot(grad_projected_low, weight_qkv.T, preferred_element_type=jnp.float32)
    input_one, gain_one, bias_one = norm_backward(
        grad_normed_one, unit_one, inverse_one, vector_full[0]
    )
    input_two, gain_two, bias_two = norm_backward(
        grad_normed_two, unit_two, inverse_two, vector_full[2]
    )
    grad_tokens = grad_rows + input_one + input_two
    grad_packed = [grad_weight_qkv, grad_weight_out, grad_weight_up]
    grad_vector = jnp.concatenate(
        [
            jnp.stack([gain_one, bias_one, gain_two, bias_two, grad_bias_rows, grad_bias_rows]),
            jnp.sum(grad_projected, axis=0).reshape(3, model_width),
            jnp.sum(grad_upward, axis=0).reshape(ffn_width // model_width, model_width),
        ],
        axis=0,
    )
    return (block_output, grad_tokens, grad_packed, grad_down, grad_vector)


def adam_moments(first_moment, second, grad_total):
    first_new = beta_first * first_moment + (1.0 - beta_first) * grad_total
    second_new = beta_second * second + (1.0 - beta_second) * grad_total * grad_total
    first_hat = first_new / (1.0 - beta_first**STEP_COUNT)
    second_hat = second_new / (1.0 - beta_second**STEP_COUNT)
    return (first_new, second_new, first_hat / (jnp.sqrt(second_hat) + adam_epsilon))


def adam_update(weight, first_moment, second, grad_total):
    first_new, second_new, direction = adam_moments(first_moment, second, grad_total)
    weight_new = weight * (1.0 - learn_rate * decay_rate) - learn_rate * direction
    return (weight_new, first_new, second_new)


def adam_change(weight, first_moment, second, grad_total):
    first_new, second_new, direction = adam_moments(first_moment, second, grad_total)
    change = -(learn_rate * decay_rate) * weight - learn_rate * direction
    return (change, first_new, second_new)


AXES = ("dp", "zero")


def exchange(value, size, mask):
    return lax.ppermute(value, AXES, [(i, i ^ mask) for i in range(size)])


def stage_lists(bit_count):
    rest = [(3, 4)] if bit_count >= 5 else [(b,) for b in range(3, bit_count)]
    rest = rest + [(b,) for b in range(5, bit_count)]
    return [[(1,), (2,)] + rest, [(2,), (1,)] + rest]


def scatter_stage(value, present, group, me, size, wire):
    span = 1 << len(group)
    low = group[0]
    mine = (me >> low) & (span - 1)
    top = group[-1]
    axis = present.index(top)
    shape = value.shape
    value = value.reshape(shape[:axis] + (span,) + shape[axis + len(group) :])
    total = lax.dynamic_index_in_dim(value, mine, axis, keepdims=False)
    for k in range(1, span):
        part = lax.dynamic_index_in_dim(value, mine ^ k, axis, keepdims=False).astype(wire)
        total = total + exchange(part, size, k << low).astype(jnp.float32)
    return total, [b for b in present if b not in group]


def scatter_parts(parts, me, size, upper=None):
    bit_count = size.bit_length() - 1
    owners = bit_count if upper is None else bit_count - 1
    rows = sum(p.shape[0] for p in parts) >> owners
    width = parts[0].shape[1]
    core = me & 1
    split = [p.reshape(p.shape[0] // (2 * rows), 2, rows, width) for p in parts]
    pieces = []
    half = width // 2
    for index, first in enumerate(((1, 2), (2, 1))):
        cut = [p[..., index * half : (index + 1) * half] for p in split]
        send = jnp.concatenate(
            [lax.dynamic_index_in_dim(p, 1 - core, 1, keepdims=False) for p in cut], axis=0
        )
        keep = jnp.concatenate(
            [lax.dynamic_index_in_dim(p, core, 1, keepdims=False) for p in cut], axis=0
        )
        value = keep + exchange(send, size, 1)
        present = list(range(owners - 1, 0, -1))
        value = value.reshape((2,) * (owners - 1) + (rows, half))
        for b in first + tuple(range(3, owners)):
            wire = jnp.bfloat16 if b in (1, 2) else jnp.float32
            value, present = scatter_stage(value, present, (b,), me, size, wire)
        if upper is not None:
            middle = size // 2
            if upper:
                pairs = [(i, i + middle) for i in range(middle)]
            else:
                pairs = [(i + middle, i) for i in range(middle)]
            value = value + lax.ppermute(value, AXES, pairs)
        pieces.append(value)
    return jnp.concatenate(pieces, axis=-1)


def gather_rows(shard, cut_row, me, size):
    rows, width = shard.shape
    bit_count = size.bit_length() - 1
    half = width // 2
    pieces = []
    for index, stages in enumerate(stage_lists(bit_count)):
        value = shard[:, index * half : (index + 1) * half]
        present = []
        for group in list(reversed(stages)) + [(0,)]:
            span = 1 << len(group)
            low = group[0]
            slots = [value] + [exchange(value, size, k << low) for k in range(1, span)]
            for t, b in enumerate(group):
                bit = ((me >> b) & 1) == 1
                slots = [jnp.where(bit, slots[j ^ (1 << t)], slots[j]) for j in range(span)]
            axis = sum(1 for b in present if b > group[-1])
            value = jnp.stack(slots, axis=axis)
            value = value.reshape(
                value.shape[:axis] + (2,) * len(group) + value.shape[axis + 1 :]
            )
            present = sorted(present + list(group), reverse=True)
        pieces.append(value.reshape(size, rows, half))
    return jnp.concatenate(
        [p[:, :cut_row].reshape(size * cut_row, half) for p in pieces], axis=-1
    ), jnp.concatenate(
        [p[:, cut_row:].reshape(size * (rows - cut_row), half) for p in pieces], axis=-1
    )


def reduce_vector(grad_vector, me, size, zero_size):
    bit_count = size.bit_length() - 1
    total = grad_vector
    for b in range(bit_count):
        total = total + exchange(total, size, 1 << b)
    width = grad_vector.shape[1] // zero_size
    return lax.dynamic_slice_in_dim(total, (me % zero_size) * width, width, axis=1)


def body(
    zero_size,
    size,
    tokens,
    cotangent,
    segment_ids,
    packed_weights,
    down_weights,
    vector_params,
    packed_first,
    packed_second,
    down_first,
    down_second,
    vector_first,
    vector_second,
):
    me = lax.axis_index("dp") * zero_size + lax.axis_index("zero")
    packed_shard = packed_weights.astype(jnp.bfloat16).T
    down_shard = down_weights.astype(jnp.bfloat16)
    vector_shard = vector_params.astype(jnp.bfloat16)
    packed_full, down_full = gather_rows(
        jnp.concatenate([packed_shard, down_shard], axis=0), packed_shard.shape[0], me, size
    )
    vector_full = lax.all_gather(vector_shard, "zero", axis=1, tiled=True)
    block_output, grad_tokens, grad_packed, grad_down, grad_vector = layer_rows(
        tokens, cotangent, segment_ids[0], packed_full, down_full, vector_full
    )
    down_sum = scatter_parts([grad_down], me, size)
    upper_sum = scatter_parts(grad_packed[2:], me, size, upper=True)
    lower_sum = scatter_parts(grad_packed[:2], me, size, upper=False)
    packed_sum = jnp.where(me >= size // 2, upper_sum, lower_sum).T
    vector_sum = reduce_vector(grad_vector, me, size, zero_size)
    packed_new, packed_first_new, packed_second_new = adam_update(
        packed_weights, packed_first, packed_second, packed_sum
    )
    down_new, down_first_new, down_second_new = adam_update(
        down_weights, down_first, down_second, down_sum
    )
    vector_step, vector_first_new, vector_second_new = adam_change(
        vector_params, vector_first, vector_second, vector_sum
    )
    return (
        block_output,
        grad_tokens,
        packed_sum,
        down_sum,
        vector_sum,
        packed_new,
        down_new,
        vector_step,
        packed_first_new,
        packed_second_new,
        down_first_new,
        down_second_new,
        vector_first_new,
        vector_second_new,
    )


def solution(mesh):
    zero_size = mesh.shape["zero"]
    size = mesh.shape["dp"] * zero_size
    return jax.shard_map(
        functools.partial(body, zero_size, size),
        mesh=mesh,
        in_specs=(
            P(("dp", "zero"), None),
            P(("dp", "zero"), None),
            P(("dp", "zero"), None),
            P(None, ("dp", "zero")),
            P(("dp", "zero"), None),
            P(None, "zero"),
            P(None, ("dp", "zero")),
            P(None, ("dp", "zero")),
            P(("dp", "zero"), None),
            P(("dp", "zero"), None),
            P(None, "zero"),
            P(None, "zero"),
        ),
        out_specs=(
            P(("dp", "zero"), None),
            P(("dp", "zero"), None),
            P(None, ("dp", "zero")),
            P(("dp", "zero"), None),
            P(None, "zero"),
            P(None, ("dp", "zero")),
            P(("dp", "zero"), None),
            P(None, "zero"),
            P(None, ("dp", "zero")),
            P(None, ("dp", "zero")),
            P(("dp", "zero"), None),
            P(("dp", "zero"), None),
            P(None, "zero"),
            P(None, "zero"),
        ),
        check_vma=False,
    )
```

```python
import functools

import jax
import jax.numpy as jnp
from jax import lax
from jax.sharding import PartitionSpec as P

H = 12
HEAD = 64
ROT = 16
STEP_COUNT = 4


norm_epsilon = 1e-05
adam_epsilon = 1e-08
learn_rate = 0.01
decay_rate = 0.1
beta_first = 0.9
beta_second = 0.95
rope_base = 10000.0
masked_value = -1e30
inv_sqrt_two = 0.7071067811865476
inv_sqrt_tau = 0.3989422804014327


def contract(form, left, right):
    return jnp.einsum(form, left, right, preferred_element_type=jnp.float32)


def layer_norm(residual, gain_vector, bias_vector):
    centered = residual - jnp.mean(residual, axis=-1, keepdims=True)
    inverse = lax.rsqrt(jnp.mean(centered * centered, axis=-1, keepdims=True) + norm_epsilon)
    normalized = centered * inverse
    return (normalized * gain_vector + bias_vector, normalized, inverse)


def norm_backward(grad_normed, normalized, inverse, gain_vector):
    grad_gain = jnp.sum(grad_normed * normalized, axis=0)
    grad_bias = jnp.sum(grad_normed, axis=0)
    grad_hat = grad_normed * gain_vector
    grad_input = inverse * (
        grad_hat
        - jnp.mean(grad_hat, axis=-1, keepdims=True)
        - normalized * jnp.mean(grad_hat * normalized, axis=-1, keepdims=True)
    )
    return (grad_input, grad_gain, grad_bias)


def rotary_tables(segment_row):
    row_count = segment_row.shape[0]
    positions_all = jnp.arange(row_count, dtype=jnp.int32)
    same_segment = segment_row[:, None] == segment_row[None, :]
    starts = jnp.min(jnp.where(same_segment, positions_all[None, :], row_count), axis=1)
    offsets = (positions_all - starts).astype(jnp.float32)
    half_rot = ROT // 2
    frequency = jnp.power(rope_base, -(jnp.arange(half_rot, dtype=jnp.float32) * 2.0 / ROT))
    angles = offsets[:, None] * frequency[None, :]
    allowed = same_segment & (positions_all[None, :] <= positions_all[:, None])
    return (jnp.cos(angles)[:, None, :], jnp.sin(angles)[:, None, :], allowed)


def rotate_heads(values, cosine, sine_table):
    half_rot = ROT // 2
    front = values[..., :half_rot]
    behind = values[..., half_rot:ROT]
    return jnp.concatenate(
        [
            front * cosine - behind * sine_table,
            behind * cosine + front * sine_table,
            values[..., ROT:],
        ],
        axis=-1,
    )


def gelu_parts(upward):
    normal_cdf = 0.5 * (1.0 + lax.erf(upward * inv_sqrt_two))
    density = jnp.exp(-0.5 * upward * upward) * inv_sqrt_tau
    return (upward * normal_cdf, normal_cdf + upward * density)


def layer_rows(me, size, token_rows, cotangent_rows, segment_row, packed_low, down_low, vector_low):
    row_count, model_width = token_rows.shape
    ffn_width = down_low.shape[0]
    vector_full = vector_low.astype(jnp.float32)
    residual = token_rows.astype(jnp.float32)
    normed_one, unit_one, inverse_one = layer_norm(residual, vector_full[0], vector_full[1])
    normed_two, unit_two, inverse_two = layer_norm(residual, vector_full[2], vector_full[3])
    normed_one_low = normed_one.astype(jnp.bfloat16)
    normed_two_low = normed_two.astype(jnp.bfloat16)
    weight_qkv = packed_low[: 3 * model_width].T
    weight_out = packed_low[3 * model_width : 4 * model_width].T
    weight_up = packed_low[4 * model_width :].T
    bias_qkv = vector_full[6:9].reshape(3 * model_width)
    bias_up = vector_full[9:].reshape(ffn_width)
    upward = jnp.dot(normed_two_low, weight_up, preferred_element_type=jnp.float32) + bias_up
    activated, gelu_slope = gelu_parts(upward)
    activated_low = activated.astype(jnp.bfloat16)
    grad_down = jnp.dot(activated_low.T, cotangent_rows, preferred_element_type=jnp.float32)
    grad_upward = (
        jnp.dot(cotangent_rows, down_low.T, preferred_element_type=jnp.float32) * gelu_slope
    )
    grad_upward_low = grad_upward.astype(jnp.bfloat16)
    grad_weight_up = jnp.dot(grad_upward_low.T, normed_two_low, preferred_element_type=jnp.float32)
    normed_one_low, grad_down, grad_weight_up = lax.optimization_barrier(
        (normed_one_low, grad_down, grad_weight_up)
    )
    chains = [
        Chain([grad_down], me, size),
        Chain([grad_weight_up], me, size, upper=True),
    ]
    projected = jnp.dot(normed_one_low, weight_qkv, preferred_element_type=jnp.float32) + bias_qkv
    heads_shape = (row_count, H, HEAD)
    cosine, sine_table, allowed = rotary_tables(segment_row)
    query_low = rotate_heads(
        projected[:, :model_width].reshape(heads_shape), cosine, sine_table
    ).astype(jnp.bfloat16)
    key_low = rotate_heads(
        projected[:, model_width : 2 * model_width].reshape(heads_shape), cosine, sine_table
    ).astype(jnp.bfloat16)
    value_low = projected[:, 2 * model_width :].reshape(heads_shape).astype(jnp.bfloat16)
    query_low, key_low, value_low = step_and_tie(chains, query_low, key_low, value_low)
    score_scale = HEAD ** (-0.5)

    def attention_scores():
        scores = contract("qhd,khd->hqk", query_low, key_low) * score_scale
        return jnp.where(allowed[None], scores, masked_value)

    scores = attention_scores()
    log_total = jnp.log(jnp.sum(jnp.exp(scores), axis=-1, keepdims=True))
    probs_low = jnp.exp(scores - log_total).astype(jnp.bfloat16)
    attended = contract("hqk,khd->qhd", probs_low, value_low)
    attended, log_total, query_low, key_low, value_low = step_and_tie(
        chains, attended, log_total, query_low, key_low, value_low
    )
    attended_low = attended.reshape(row_count, model_width).astype(jnp.bfloat16)
    branch_attn = (
        jnp.dot(attended_low, weight_out, preferred_element_type=jnp.float32) + vector_full[4]
    )
    branch_mlp = (
        jnp.dot(activated_low, down_low, preferred_element_type=jnp.float32) + vector_full[5]
    )
    block_output = (residual + branch_attn + branch_mlp).astype(jnp.bfloat16)
    grad_rows = cotangent_rows.astype(jnp.float32)
    grad_bias_rows = jnp.sum(grad_rows, axis=0)
    grad_normed_two = jnp.dot(grad_upward_low, weight_up.T, preferred_element_type=jnp.float32)
    grad_weight_out = jnp.dot(cotangent_rows.T, attended_low, preferred_element_type=jnp.float32)
    grad_attended_low = (
        jnp.dot(cotangent_rows, weight_out.T, preferred_element_type=jnp.float32)
        .astype(jnp.bfloat16)
        .reshape(heads_shape)
    )
    correction = jnp.sum(grad_attended_low.astype(jnp.float32) * attended, axis=-1)
    attention_probs = jnp.exp(attention_scores() - log_total)
    grad_probs = contract("qhd,khd->hqk", grad_attended_low, value_low)
    grad_scores_low = (
        attention_probs * (grad_probs - correction.T[:, :, None]) * score_scale
    ).astype(jnp.bfloat16)
    probs_again = attention_probs.astype(jnp.bfloat16)
    grad_query = contract("hqk,khd->qhd", grad_scores_low, key_low)
    grad_key = contract("hqk,qhd->khd", grad_scores_low, query_low)
    grad_value = contract("hqk,qhd->khd", probs_again, grad_attended_low)
    grad_query, grad_key, grad_value = step_and_tie(chains, grad_query, grad_key, grad_value)
    grad_projected = jnp.concatenate(
        [
            rotate_heads(grad_query, cosine, -sine_table).reshape(row_count, model_width),
            rotate_heads(grad_key, cosine, -sine_table).reshape(row_count, model_width),
            grad_value.reshape(row_count, model_width),
        ],
        axis=1,
    )
    grad_projected_low = grad_projected.astype(jnp.bfloat16)
    grad_weight_qkv = jnp.dot(
        grad_projected_low.T, normed_one_low, preferred_element_type=jnp.float32
    )
    grad_normed_one = jnp.dot(grad_projected_low, weight_qkv.T, preferred_element_type=jnp.float32)
    input_one, gain_one, bias_one = norm_backward(
        grad_normed_one, unit_one, inverse_one, vector_full[0]
    )
    input_two, gain_two, bias_two = norm_backward(
        grad_normed_two, unit_two, inverse_two, vector_full[2]
    )
    grad_tokens = grad_rows + input_one + input_two
    grad_packed = [grad_weight_qkv, grad_weight_out]
    grad_vector = jnp.concatenate(
        [
            jnp.stack([gain_one, bias_one, gain_two, bias_two, grad_bias_rows, grad_bias_rows]),
            jnp.sum(grad_projected, axis=0).reshape(3, model_width),
            jnp.sum(grad_upward, axis=0).reshape(ffn_width // model_width, model_width),
        ],
        axis=0,
    )
    return (block_output, grad_tokens, grad_packed, chains, grad_vector)


def adam_moments(first_moment, second, grad_total):
    first_new = beta_first * first_moment + (1.0 - beta_first) * grad_total
    second_new = beta_second * second + (1.0 - beta_second) * grad_total * grad_total
    first_hat = first_new / (1.0 - beta_first**STEP_COUNT)
    second_hat = second_new / (1.0 - beta_second**STEP_COUNT)
    return (first_new, second_new, first_hat / (jnp.sqrt(second_hat) + adam_epsilon))


def adam_update(weight, first_moment, second, grad_total):
    first_new, second_new, direction = adam_moments(first_moment, second, grad_total)
    weight_new = weight * (1.0 - learn_rate * decay_rate) - learn_rate * direction
    return (weight_new, first_new, second_new)


def adam_change(weight, first_moment, second, grad_total):
    first_new, second_new, direction = adam_moments(first_moment, second, grad_total)
    change = -(learn_rate * decay_rate) * weight - learn_rate * direction
    return (change, first_new, second_new)


AXES = ("dp", "zero")


def exchange(value, size, mask):
    return lax.ppermute(value, AXES, [(i, i ^ mask) for i in range(size)])


def stage_lists(bit_count):
    rest = [(3, 4)] if bit_count >= 5 else [(b,) for b in range(3, bit_count)]
    rest = rest + [(b,) for b in range(5, bit_count)]
    return [[(1,), (2,)] + rest, [(2,), (1,)] + rest]


def scatter_stage(value, present, group, me, size, wire):
    span = 1 << len(group)
    low = group[0]
    mine = (me >> low) & (span - 1)
    top = group[-1]
    axis = present.index(top)
    shape = value.shape
    value = value.reshape(shape[:axis] + (span,) + shape[axis + len(group) :])
    total = lax.dynamic_index_in_dim(value, mine, axis, keepdims=False)
    for k in range(1, span):
        part = lax.dynamic_index_in_dim(value, mine ^ k, axis, keepdims=False).astype(wire)
        total = total + exchange(part, size, k << low).astype(jnp.float32)
    return total, [b for b in present if b not in group]


class Chain:
    def __init__(self, parts, me, size, upper=None):
        self.me, self.size, self.upper = me, size, upper
        bit_count = size.bit_length() - 1
        self.owners = bit_count if upper is None else bit_count - 1
        self.rows = sum(p.shape[0] for p in parts) >> self.owners
        self.half = parts[0].shape[1] // 2
        self.split = [p.reshape(p.shape[0] // (2 * self.rows), 2, self.rows, -1) for p in parts]
        self.values = []
        self.present = [list(range(self.owners - 1, 0, -1)) for _ in range(2)]
        self.orders = [first + tuple(range(3, self.owners)) for first in ((1, 2), (2, 1))]
        self.place = -1

    def first(self, index):
        core = self.me & 1
        cut = [p[..., index * self.half : (index + 1) * self.half] for p in self.split]
        send, keep = (
            jnp.concatenate(
                [lax.dynamic_index_in_dim(p, c, 1, keepdims=False) for p in cut], axis=0
            )
            for c in (1 - core, core)
        )
        value = keep + exchange(send, self.size, 1)
        return value.reshape((2,) * (self.owners - 1) + (self.rows, self.half))

    def step(self):
        if self.place < 0:
            self.values = [self.first(index) for index in range(2)]
        elif self.place < len(self.orders[0]):
            for index in range(2):
                b = self.orders[index][self.place]
                wire = jnp.bfloat16 if b in (1, 2) else jnp.float32
                self.values[index], self.present[index] = scatter_stage(
                    self.values[index], self.present[index], (b,), self.me, self.size, wire
                )
        elif self.upper is not None:
            middle = self.size // 2
            if self.upper:
                pairs = [(i, i + middle) for i in range(middle)]
            else:
                pairs = [(i + middle, i) for i in range(middle)]
            self.values = [v + lax.ppermute(v, AXES, pairs) for v in self.values]
        self.place += 1

    def finish(self):
        while self.place <= len(self.orders[0]):
            self.step()
        return jnp.concatenate(self.values, axis=-1)


def step_and_tie(chains, *arrays):
    for chain in chains:
        chain.step()
    held, arrays = lax.optimization_barrier(([chain.values for chain in chains], arrays))
    for chain, values in zip(chains, held):
        chain.values = list(values)
    return arrays


def gather_rows(shard, me, size):
    rows, width = shard.shape
    bit_count = size.bit_length() - 1
    half = width // 2
    pieces = []
    for index, stages in enumerate(stage_lists(bit_count)):
        value = shard[:, index * half : (index + 1) * half]
        present = []
        for group in list(reversed(stages)) + [(0,)]:
            span = 1 << len(group)
            low = group[0]
            slots = [value] + [exchange(value, size, k << low) for k in range(1, span)]
            for t, b in enumerate(group):
                bit = ((me >> b) & 1) == 1
                slots = [jnp.where(bit, slots[j ^ (1 << t)], slots[j]) for j in range(span)]
            axis = sum(1 for b in present if b > group[-1])
            value = jnp.stack(slots, axis=axis)
            value = value.reshape(
                value.shape[:axis] + (2,) * len(group) + value.shape[axis + 1 :]
            )
            present = sorted(present + list(group), reverse=True)
        pieces.append(value.reshape(size * rows, half))
    return jnp.concatenate(pieces, axis=-1)


def reduce_vector(grad_vector, me, size, zero_size):
    bit_count = size.bit_length() - 1
    total = grad_vector
    for b in range(bit_count):
        total = total + exchange(total, size, 1 << b)
    width = grad_vector.shape[1] // zero_size
    return lax.dynamic_slice_in_dim(total, (me % zero_size) * width, width, axis=1)


def body(
    zero_size,
    size,
    tokens,
    cotangent,
    segment_ids,
    packed_weights,
    down_weights,
    vector_params,
    packed_first,
    packed_second,
    down_first,
    down_second,
    vector_first,
    vector_second,
):
    me = lax.axis_index("dp") * zero_size + lax.axis_index("zero")
    packed_shard = packed_weights.astype(jnp.bfloat16).T
    down_shard = down_weights.astype(jnp.bfloat16)
    vector_shard = vector_params.astype(jnp.bfloat16)
    packed_full = gather_rows(packed_shard, me, size)
    down_full = gather_rows(down_shard, me, size)
    vector_full = lax.all_gather(vector_shard, "zero", axis=1, tiled=True)
    block_output, grad_tokens, grad_packed, chains, grad_vector = layer_rows(
        me, size, tokens, cotangent, segment_ids[0], packed_full, down_full, vector_full
    )
    down_sum, upper_sum = (chain.finish() for chain in chains)
    lower_sum = Chain(grad_packed, me, size, upper=False).finish()
    packed_sum = jnp.where(me >= size // 2, upper_sum, lower_sum).T
    vector_sum = reduce_vector(grad_vector, me, size, zero_size)
    packed_new, packed_first_new, packed_second_new = adam_update(
        packed_weights, packed_first, packed_second, packed_sum
    )
    down_new, down_first_new, down_second_new = adam_update(
        down_weights, down_first, down_second, down_sum
    )
    vector_step, vector_first_new, vector_second_new = adam_change(
        vector_params, vector_first, vector_second, vector_sum
    )
    return (
        block_output,
        grad_tokens,
        packed_sum,
        down_sum,
        vector_sum,
        packed_new,
        down_new,
        vector_step,
        packed_first_new,
        packed_second_new,
        down_first_new,
        down_second_new,
        vector_first_new,
        vector_second_new,
    )


def solution(mesh):
    zero_size = mesh.shape["zero"]
    size = mesh.shape["dp"] * zero_size
    return jax.shard_map(
        functools.partial(body, zero_size, size),
        mesh=mesh,
        in_specs=(
            P(("dp", "zero"), None),
            P(("dp", "zero"), None),
            P(("dp", "zero"), None),
            P(None, ("dp", "zero")),
            P(("dp", "zero"), None),
            P(None, "zero"),
            P(None, ("dp", "zero")),
            P(None, ("dp", "zero")),
            P(("dp", "zero"), None),
            P(("dp", "zero"), None),
            P(None, "zero"),
            P(None, "zero"),
        ),
        out_specs=(
            P(("dp", "zero"), None),
            P(("dp", "zero"), None),
            P(None, ("dp", "zero")),
            P(("dp", "zero"), None),
            P(None, "zero"),
            P(None, ("dp", "zero")),
            P(("dp", "zero"), None),
            P(None, "zero"),
            P(None, ("dp", "zero")),
            P(None, ("dp", "zero")),
            P(("dp", "zero"), None),
            P(("dp", "zero"), None),
            P(None, "zero"),
            P(None, "zero"),
        ),
        check_vma=False,
    )
```
